512 devices in a mesh: row: 32 (over z, core), col: 16 (over y, x).
Axes of the slice: x: 4, y: 4, z: 16, core: 2. Of those that a mesh axis runs over, the one named last changes fastest.
Arguments:
- noise: bfloat16 [4096, 16384], P('row', 'col'), may hold values from -6 to 6
- data: bfloat16 [4096, 16384], P('col', 'row'), may hold values from -6 to 6
Outputs:
- targets: bfloat16 [4096, 16384], P('row', 'col')
- noise_potential: float32 [4096], P('row')
- data_potential: float32 [4096], P('col')
The draws below stay inside these ranges and needn't reach their ends.
All inputs are finite; a program needn't handle non-finite values.
Results may differ from the reference program's by a relative error of at most 0.017.
Values may be sent and summed in bfloat16 or wider, within the bound.
No kernel may reach another device: no remote copies, remote signals or barrier semaphores. Data moves between devices by JAX's collectives and lax.ppermute only.
A program may use at most 64 MiB of HBM per device.

```python
import jax
import jax.numpy as jnp
from jax import lax

DL = 16384
COLS_DEV = 256
ITERS = 3
NN = 4096
NM = 4096
N_COL = 16


pair_count = 4


def paired_rows(key, strength, offset):
    key_rows = jax.random.fold_in(key, 11)
    key_cols = jax.random.fold_in(key, 12)
    key_anchor = jax.random.fold_in(key, 13)
    key_closest = jax.random.fold_in(key, 14)
    key_runner = jax.random.fold_in(key, 15)
    noise_slots = jax.random.permutation(key_rows, NN)[:pair_count]
    data_slots = jax.random.permutation(key_cols, NM)[:2 * pair_count]
    ladder = jnp.arange(pair_count, dtype=jnp.float32)
    scales = strength + offset * ladder
    anchor = jnp.clip(jax.random.normal(key_anchor, (pair_count, DL), jnp.float32), -2.5, 2.5) * scales[:, None]
    closest_sign = jax.random.rademacher(key_closest, (pair_count, DL), jnp.float32)
    runner_sign = jax.random.rademacher(key_runner, (pair_count, DL), jnp.float32)
    runner_reach = jnp.sqrt(0.0225 + 0.01 * (1.0 + jnp.mod(ladder, 3.0)))
    closest = anchor + 0.15 * closest_sign
    runner_up = anchor + runner_reach[:, None] * runner_sign
    return (noise_slots, data_slots, anchor, closest, runner_up)


def scaled_rows(key, count, lowest, highest):
    key_scale = jax.random.fold_in(key, 21)
    key_values = jax.random.fold_in(key, 22)
    spread = jnp.exp(jax.random.uniform(key_scale, (count, 1), jnp.float32, jnp.log(lowest), jnp.log(highest)))
    return jnp.clip(jax.random.normal(key_values, (count, DL), jnp.float32), -3.5, 3.5) * spread


def draw_noise(key, part):
    strength, offset, lowest, highest = (1.0, 0.3, 0.9, 1.25)
    noise_slots, data_slots, anchor, closest, runner_up = paired_rows(key, strength, offset)
    key = jax.random.fold_in(key, 3)
    values = scaled_rows(key, NN, lowest, highest)
    values = values.at[noise_slots].set(anchor)
    return values.astype(jnp.bfloat16)


def draw_data(key, part):
    strength, offset, lowest, highest = (1.0, 0.3, 0.9, 1.2)
    noise_slots, data_slots, anchor, closest, runner_up = paired_rows(key, strength, offset)
    key = jax.random.fold_in(key, 5)
    values = scaled_rows(key, NM, lowest, highest)
    values = values.at[data_slots[:pair_count]].set(closest)
    values = values.at[data_slots[pair_count:]].set(runner_up)
    return values.astype(jnp.bfloat16)


def setup_inputs(seed: int = 0) -> dict:
    keys = jax.random.split(jax.random.key(seed), 3)
    noise = draw_noise(jax.random.fold_in(keys[2], 71), 0)
    data = draw_data(jax.random.fold_in(keys[2], 71), 0)
    return {"noise": noise, "data": data}


epsilon = 0.01


def log_sum_exp(scores, axis):
    peak = jnp.max(scores, axis=axis, keepdims=True)
    total = jnp.sum(jnp.exp(scores - peak), axis=axis)
    return jnp.squeeze(peak, axis) + jnp.log(total)


def reference(noise, data):
    noise_sq = jnp.einsum("id,id->i", noise, noise, preferred_element_type=jnp.float32)
    data_sq = jnp.einsum("jd,jd->j", data, data, preferred_element_type=jnp.float32)
    dots = lax.dot_general(noise, data, (((1,), (1,)), ((), ())), preferred_element_type=jnp.float32)
    cost = (noise_sq[:, None] + data_sq[None, :] - 2.0 * dots) / DL
    data_potential = jnp.zeros((NM,), jnp.float32)
    log_rows = jnp.log(jnp.float32(NN))
    log_cols = jnp.log(jnp.float32(NM))
    noise_potential = jnp.zeros((NN,), jnp.float32)
    for step in range(ITERS):
        noise_potential = epsilon * (-log_rows - log_sum_exp((data_potential[None, :] - cost) / epsilon, 1))
        data_potential = epsilon * (-log_cols - log_sum_exp((noise_potential[:, None] - cost) / epsilon, 0))
    plan = jnp.exp((noise_potential[:, None] + data_potential[None, :] - cost) / epsilon + log_rows).astype(jnp.bfloat16)
    mass = jnp.sum(plan.astype(jnp.float32), axis=1)
    plan_blocks = plan.reshape(NN, N_COL, COLS_DEV).transpose(1, 0, 2)
    data_blocks = data.reshape(N_COL, COLS_DEV, DL)

    def accumulate(total, pair):
        block_plan, block_data = pair
        partial_value = jnp.dot(block_plan, block_data, preferred_element_type=jnp.float32).astype(jnp.bfloat16)
        partial_value = lax.optimization_barrier(partial_value)
        return total + partial_value.astype(jnp.float32), None

    weighted, unused = lax.scan(accumulate, jnp.zeros((NN, DL), jnp.float32), (plan_blocks, data_blocks))
    targets = (weighted / mass[:, None]).astype(jnp.bfloat16)
    return targets, noise_potential, data_potential
```

```python
import functools
import math

import jax
import jax.numpy as jnp
from jax import lax
from jax.experimental import pallas as pl
from jax.experimental.pallas import tpu as pltpu
from jax.sharding import PartitionSpec as P

ITERS = 3
EPS = 0.01
COLS = 16
ROWS = 32
F32 = jnp.float32
BF16 = jnp.bfloat16
GRID = 4
MIB = 1024 * 1024


def copies(value, axis, size):
    sent = jnp.broadcast_to(value[None], (size,) + value.shape)
    return lax.all_to_all(sent, axis, split_axis=0, concat_axis=0)


def fold(value):
    value = value.astype(F32)
    value = value * value
    parts = [value[..., k : k + 128] for k in range(0, value.shape[-1], 128)]
    while len(parts) > 1:
        parts = [parts[k] + parts[k + 1] for k in range(0, len(parts), 2)]
    return parts[0]


def split(value):
    parts = []
    for _ in range(2):
        far = value * 65537.0
        head = far - (far - value)
        parts.append(head)
        value = value - head
    return parts + [value]


def cost_kernel(scale, place_ref, noise_ref, data_ref, noise_sq_ref, cost_ref, pack_ref, dots_ref, data_sq_ref):
    step = pl.program_id(0)
    core, plane = place_ref[0], place_ref[1]
    blocks, rows, _ = noise_ref.shape
    depth = data_ref.shape[2]
    part = pack_ref.shape[1]

    @pl.when(step == 0)
    def _():
        dots_ref[...] = jnp.zeros_like(dots_ref)
        data_sq_ref[...] = jnp.zeros_like(data_sq_ref)

    dots, data_sq = dots_ref[...], data_sq_ref[...]
    for b in range(blocks):
        for k in range(2):
            data = data_ref[2 * b + k]
            noise = noise_ref[b, :, k * depth : (k + 1) * depth]
            dots += lax.dot_general(noise, data, (((1,), (1,)), ((), ())), preferred_element_type=F32)
            data_sq += fold(data)
        here = pl.ds(pl.multiple_of(plane * part, part), part)
        pack_ref[step * blocks + b, :, :depth] = data_ref[2 * b + core, here, :]
    dots_ref[...], data_sq_ref[...] = dots, data_sq

    @pl.when(step == pl.num_programs(0) - 1)
    def _():
        squares = jnp.sum(noise_sq_ref[...], axis=1, keepdims=True) + jnp.sum(data_sq.T, axis=0, keepdims=True)
        cost = squares - 2.0 * dots
        cost_ref[...] = cost
        scores = cost * scale
        peak = jnp.max(scores, axis=1, keepdims=True)
        local = peak + jnp.log(jnp.sum(jnp.exp(scores - peak), axis=1, keepdims=True))
        line = jnp.broadcast_to(local, (rows, 128)).T[:part, :]
        place = lax.broadcasted_iota(jnp.int32, line.shape, 0)
        head, middle, rest = split(line)
        tail = jnp.where(place == 0, head, jnp.where(place == 1, middle, rest)).astype(BF16)
        for c in range(pack_ref.shape[0]):
            pack_ref[c, :, depth:] = tail


def plan_kernel(plan_ref, data_ref, out_ref, acc_ref, mass_ref):
    step = pl.program_id(0)
    parts, cores, blocks, _, width = data_ref.shape

    @pl.when(step == 0)
    def _():
        acc_ref[...] = jnp.zeros_like(acc_ref)
        mass_ref[...] = jnp.zeros_like(mass_ref)

    for b in range(blocks):
        plan = plan_ref[b]
        mass_ref[...] += jnp.sum(plan.astype(F32), axis=1, keepdims=True)
        for k in range(cores):
            block = jnp.concatenate([data_ref[s, k, b] for s in range(parts)], axis=0)
            acc_ref[:, k * width : (k + 1) * width] += jnp.dot(plan, block, preferred_element_type=F32)

    @pl.when(step == pl.num_programs(0) - 1)
    def _():
        out_ref[...] = (acc_ref[...] / mass_ref[...]).astype(BF16)


def log_sum_exp(value, axis):
    peak = jnp.max(value, axis=axis, keepdims=True)
    return jnp.squeeze(peak, axis) + jnp.log(jnp.sum(jnp.exp(value - peak), axis=axis))


def body(noise, data):
    rows, width = noise.shape
    cols, depth = data.shape
    planes = ROWS // 2
    part = cols // planes
    log_rows = math.log(rows * ROWS)
    log_cols = math.log(cols * COLS)
    scale = -1.0 / (EPS * width * COLS)
    row = lax.axis_index("row").astype(jnp.int32)
    place = jnp.stack([lax.rem(row, 2), row // 2])

    data_all = lax.all_gather(data, "row", axis=0)
    noise_all = copies(noise, "col", COLS)
    noise_sq = fold(noise_all).sum(axis=0)
    data_all, noise_all, noise_sq = lax.optimization_barrier((data_all, noise_all, noise_sq))

    some = COLS // GRID
    cost, pack = pl.pallas_call(
        functools.partial(cost_kernel, scale),
        out_shape=[
            jax.ShapeDtypeStruct((rows, cols), F32),
            jax.ShapeDtypeStruct((COLS, part, depth + rows), BF16),
        ],
        grid_spec=pltpu.PrefetchScalarGridSpec(
            num_scalar_prefetch=1,
            grid=(GRID,),
            in_specs=[
                pl.BlockSpec((some, rows, width), lambda c, place: (c, 0, 0)),
                pl.BlockSpec((2 * some, cols, depth), lambda c, place: (c, 0, 0)),
                pl.BlockSpec((rows, 128), lambda c, place: (0, 0)),
            ],
            out_specs=[
                pl.BlockSpec((rows, cols), lambda c, place: (0, 0)),
                pl.BlockSpec((COLS, part, depth + rows), lambda c, place: (0, 0, 0)),
            ],
            scratch_shapes=[
                pltpu.VMEM((rows, cols), F32),
                pltpu.VMEM((cols, 128), F32),
            ],
        ),
        compiler_params=pltpu.CompilerParams(vmem_limit_bytes=48 * MIB),
        cost_estimate=pl.CostEstimate(
            flops=2 * rows * cols * COLS * width, bytes_accessed=12 * MIB, transcendentals=0
        ),
        name="cost",
    )(place, noise_all, data_all, noise_sq)
    scores = cost * scale
    pack = lax.all_to_all(pack, "col", split_axis=0, concat_axis=0)
    parts = pack[:, :3, depth:].astype(F32).sum(axis=1)

    values = lax.all_gather(pack[:, :, :depth], "row", axis=0).reshape(planes, 2, COLS, part, depth)

    for step in range(ITERS):
        if step > 0:
            parts = copies(log_sum_exp(scores + v[None, :], 1).reshape(1, rows), "col", COLS)
        u = -log_rows - log_sum_exp(parts.reshape(COLS, rows), 0)
        local = log_sum_exp(scores + u[:, None], 0)
        parts = copies(local.reshape(1, cols), "row", ROWS)
        v = -log_cols - log_sum_exp(parts, 0).reshape(cols)

    values, v = lax.optimization_barrier((values, v))
    plan = jnp.exp(scores + u[:, None] + v[None, :] + log_rows).astype(BF16)
    plan = copies(plan, "col", COLS)
    targets = pl.pallas_call(
        plan_kernel,
        grid=(GRID,),
        out_shape=jax.ShapeDtypeStruct((rows, width), BF16),
        in_specs=[
            pl.BlockSpec((some, rows, cols), lambda c: (c, 0, 0)),
            pl.BlockSpec((planes, 2, some, part, depth), lambda c: (0, 0, c, 0, 0)),
        ],
        out_specs=pl.BlockSpec((rows, width), lambda c: (0, 0)),
        scratch_shapes=[pltpu.VMEM((rows, width), F32), pltpu.VMEM((rows, 1), F32)],
        compiler_params=pltpu.CompilerParams(vmem_limit_bytes=48 * MIB),
        name="plan",
    )(plan, values)
    return (targets, EPS * u, EPS * v)


def solution(mesh):
    return jax.shard_map(
        body,
        mesh=mesh,
        in_specs=(P("row", "col"), P("col", "row")),
        out_specs=(P("row", "col"), P("row"), P("col")),
        check_vma=False,
    )
```

```python
import functools
import math

import jax
import jax.numpy as jnp
from jax import lax
from jax.experimental import pallas as pl
from jax.experimental.pallas import tpu as pltpu
from jax.sharding import PartitionSpec as P

ITERS = 3
EPS = 0.01
COLS = 16
ROWS = 32
F32 = jnp.float32
BF16 = jnp.bfloat16
GRID = 4
MIB = 1024 * 1024


def copies(value, axis, size):
    sent = jnp.broadcast_to(value[None], (size,) + value.shape)
    return lax.all_to_all(sent, axis, split_axis=0, concat_axis=0)


def fold(value):
    value = value.astype(F32)
    value = value * value
    parts = [value[..., k : k + 128] for k in range(0, value.shape[-1], 128)]
    while len(parts) > 1:
        parts = [parts[k] + parts[k + 1] for k in range(0, len(parts), 2)]
    return parts[0]


def split(value):
    parts = []
    for _ in range(2):
        far = value * 65537.0
        head = far - (far - value)
        parts.append(head)
        value = value - head
    return parts + [value]


def cost_kernel(scale, place_ref, noise_ref, data_ref, noise_sq_ref, cost_ref, pack_ref, dots_ref, data_sq_ref):
    step = pl.program_id(0)
    core, plane = place_ref[0], place_ref[1]
    blocks, _, rows = noise_ref.shape
    depth = data_ref.shape[2]
    part = pack_ref.shape[1]

    @pl.when(step == 0)
    def _():
        dots_ref[...] = jnp.zeros_like(dots_ref)
        data_sq_ref[...] = jnp.zeros_like(data_sq_ref)

    dots, data_sq = dots_ref[...], data_sq_ref[...]
    for b in range(blocks):
        for k in range(2):
            data = data_ref[2 * b + k]
            noise = noise_ref[b, k * depth : (k + 1) * depth, :]
            dots += jnp.dot(data, noise, preferred_element_type=F32)
            data_sq += fold(data)
        here = pl.ds(pl.multiple_of(plane * part, part), part)
        pack_ref[step * blocks + b, :, :depth] = data_ref[2 * b + core, here, :]
    dots_ref[...], data_sq_ref[...] = dots, data_sq

    @pl.when(step == pl.num_programs(0) - 1)
    def _():
        squares = jnp.sum(data_sq, axis=1, keepdims=True) + noise_sq_ref[...]
        turned = squares - 2.0 * dots
        cost_ref[...] = turned.T
        scores = turned * scale
        peak = jnp.max(scores, axis=0, keepdims=True)
        local = peak + jnp.log(jnp.sum(jnp.exp(scores - peak), axis=0, keepdims=True))
        line = jnp.broadcast_to(local, (part, rows))
        place = lax.broadcasted_iota(jnp.int32, line.shape, 0)
        head, middle, rest = split(line)
        tail = jnp.where(place == 0, head, jnp.where(place == 1, middle, rest)).astype(BF16)
        for c in range(pack_ref.shape[0]):
            pack_ref[c, :, depth:] = tail


def stage_kernel(data_ref, out_ref):
    parts, cores, blocks, part, depth = data_ref.shape
    for b in range(blocks):
        for s in range(parts):
            for k in range(cores):
                out_ref[b, s * part : (s + 1) * part, k * depth : (k + 1) * depth] = data_ref[s, k, b]


def plan_kernel(plan_ref, data_ref, out_ref, acc_ref, mass_ref):
    step = pl.program_id(0)

    @pl.when(step == 0)
    def _():
        acc_ref[...] = jnp.zeros_like(acc_ref)
        mass_ref[...] = jnp.zeros_like(mass_ref)

    for b in range(plan_ref.shape[0]):
        plan = plan_ref[b]
        mass_ref[...] += jnp.sum(plan.astype(F32), axis=1, keepdims=True)
        acc_ref[...] += jnp.dot(plan, data_ref[b], preferred_element_type=F32)

    @pl.when(step == pl.num_programs(0) - 1)
    def _():
        out_ref[...] = (acc_ref[...] / mass_ref[...]).astype(BF16)


def log_sum_exp(value, axis):
    peak = jnp.max(value, axis=axis, keepdims=True)
    return jnp.squeeze(peak, axis) + jnp.log(jnp.sum(jnp.exp(value - peak), axis=axis))


def body(noise, data):
    rows, width = noise.shape
    cols, depth = data.shape
    planes = ROWS // 2
    part = cols // planes
    log_rows = math.log(rows * ROWS)
    log_cols = math.log(cols * COLS)
    scale = -1.0 / (EPS * width * COLS)
    row = lax.axis_index("row").astype(jnp.int32)
    place = jnp.stack([lax.rem(row, 2), row // 2])

    data_all = lax.all_gather(data, "row", axis=0)
    noise_all = copies(noise.T, "col", COLS)
    noise_sq = jnp.sum(jnp.square(noise_all.astype(F32)), axis=(0, 1)).reshape(1, rows)
    data_all, noise_all, noise_sq = lax.optimization_barrier((data_all, noise_all, noise_sq))

    some = COLS // GRID
    cost, pack = pl.pallas_call(
        functools.partial(cost_kernel, scale),
        out_shape=[
            jax.ShapeDtypeStruct((rows, cols), F32),
            jax.ShapeDtypeStruct((COLS, part, depth + rows), BF16),
        ],
        grid_spec=pltpu.PrefetchScalarGridSpec(
            num_scalar_prefetch=1,
            grid=(GRID,),
            in_specs=[
                pl.BlockSpec((some, width, rows), lambda c, place: (c, 0, 0)),
                pl.BlockSpec((2 * some, cols, depth), lambda c, place: (c, 0, 0)),
                pl.BlockSpec((1, rows), lambda c, place: (0, 0)),
            ],
            out_specs=[
                pl.BlockSpec((rows, cols), lambda c, place: (0, 0)),
                pl.BlockSpec((COLS, part, depth + rows), lambda c, place: (0, 0, 0)),
            ],
            scratch_shapes=[
                pltpu.VMEM((cols, rows), F32),
                pltpu.VMEM((cols, 128), F32),
            ],
        ),
        compiler_params=pltpu.CompilerParams(vmem_limit_bytes=48 * MIB),
        cost_estimate=pl.CostEstimate(
            flops=2 * rows * cols * COLS * width, bytes_accessed=12 * MIB, transcendentals=0
        ),
        name="cost",
    )(place, noise_all, data_all, noise_sq)
    scores = cost * scale
    pack = lax.all_to_all(pack, "col", split_axis=0, concat_axis=0)
    parts = pack[:, :3, depth:].astype(F32).sum(axis=1)

    values = lax.all_gather(pack[:, :, :depth], "row", axis=0).reshape(planes, 2, COLS, part, depth)

    for step in range(ITERS):
        if step > 0:
            parts = copies(log_sum_exp(scores + v[None, :], 1).reshape(1, rows), "col", COLS)
        u = -log_rows - log_sum_exp(parts.reshape(COLS, rows), 0)
        local = log_sum_exp(scores + u[:, None], 0)
        parts = copies(local.reshape(1, cols), "row", ROWS)
        v = -log_cols - log_sum_exp(parts, 0).reshape(cols)

    plan = jnp.exp(scores + u[:, None] + v[None, :] + log_rows).astype(BF16)
    plan = jnp.broadcast_to(plan[None], (COLS, rows, cols))
    values, plan = lax.optimization_barrier((values, plan))
    plan = lax.all_to_all(plan, "col", split_axis=0, concat_axis=0)
    staged = pl.pallas_call(
        stage_kernel,
        grid=(GRID,),
        out_shape=jax.ShapeDtypeStruct((COLS, cols, width), BF16),
        in_specs=[pl.BlockSpec((planes, 2, some, part, depth), lambda c: (0, 0, c, 0, 0))],
        out_specs=pl.BlockSpec((some, cols, width), lambda c: (c, 0, 0)),
        compiler_params=pltpu.CompilerParams(vmem_limit_bytes=50 * MIB),
        cost_estimate=pl.CostEstimate(flops=0, bytes_accessed=16 * MIB, transcendentals=0),
        name="stage",
    )(values)
    targets = pl.pallas_call(
        plan_kernel,
        grid=(GRID,),
        out_shape=jax.ShapeDtypeStruct((rows, width), BF16),
        in_specs=[
            pl.BlockSpec((some, rows, cols), lambda c: (c, 0, 0)),
            pl.BlockSpec((some, cols, width), lambda c: (c, 0, 0)),
        ],
        out_specs=pl.BlockSpec((rows, width), lambda c: (0, 0)),
        scratch_shapes=[pltpu.VMEM((rows, width), F32), pltpu.VMEM((rows, 1), F32)],
        compiler_params=pltpu.CompilerParams(vmem_limit_bytes=24 * MIB),
        name="plan",
    )(plan, staged)
    return (targets, EPS * u, EPS * v)


def solution(mesh):
    return jax.shard_map(
        body,
        mesh=mesh,
        in_specs=(P("row", "col"), P("col", "row")),
        out_specs=(P("row", "col"), P("row"), P("col")),
        check_vma=False,
    )
```

```python
import functools
import math

import jax
import jax.numpy as jnp
from jax import lax
from jax.experimental import pallas as pl
from jax.experimental.pallas import tpu as pltpu
from jax.sharding import PartitionSpec as P

ITERS = 3
EPS = 0.01
COLS = 16
ROWS = 32
F32 = jnp.float32
BF16 = jnp.bfloat16
GRID = 4
MIB = 1024 * 1024
VM = pl.BlockSpec(memory_space=pltpu.VMEM)


def copies(value, axis, size):
    sent = jnp.broadcast_to(value[None], (size,) + value.shape)
    return lax.all_to_all(sent, axis, split_axis=0, concat_axis=0)


def fold(value):
    value = value.astype(F32)
    value = value * value
    parts = [value[..., k : k + 128] for k in range(0, value.shape[-1], 128)]
    while len(parts) > 1:
        parts = [parts[k] + parts[k + 1] for k in range(0, len(parts), 2)]
    return parts[0]


def split(value):
    parts = []
    for _ in range(2):
        far = value * 65537.0
        head = far - (far - value)
        parts.append(head)
        value = value - head
    return parts + [value]


def cost_kernel(scale, place_ref, noise_ref, data_ref, noise_sq_ref, cost_ref, pack_ref, dots_ref, data_sq_ref):
    step = pl.program_id(0)
    core, plane = place_ref[0], place_ref[1]
    blocks, rows = data_ref.shape[0] // 2, noise_ref.shape[2]
    depth = data_ref.shape[2]
    part = pack_ref.shape[1]

    @pl.when(step == 0)
    def _():
        dots_ref[...] = jnp.zeros_like(dots_ref)
        data_sq_ref[...] = jnp.zeros_like(data_sq_ref)

    dots, data_sq = dots_ref[...], data_sq_ref[...]
    for b in range(blocks):
        for k in range(2):
            data = data_ref[2 * b + k]
            noise = noise_ref[step * blocks + b, k * depth : (k + 1) * depth, :]
            dots += jnp.dot(data, noise, preferred_element_type=F32)
            data_sq += fold(data)
        here = pl.ds(pl.multiple_of(plane * part, part), part)
        pack_ref[step * blocks + b, :, :depth] = data_ref[2 * b + core, here, :]
    dots_ref[...], data_sq_ref[...] = dots, data_sq

    @pl.when(step == pl.num_programs(0) - 1)
    def _():
        squares = jnp.sum(data_sq, axis=1, keepdims=True) + noise_sq_ref[...]
        turned = squares - 2.0 * dots
        cost_ref[...] = turned.T
        scores = turned * scale
        peak = jnp.max(scores, axis=0, keepdims=True)
        local = peak + jnp.log(jnp.sum(jnp.exp(scores - peak), axis=0, keepdims=True))
        line = jnp.broadcast_to(local, (part, rows))
        place = lax.broadcasted_iota(jnp.int32, line.shape, 0)
        head, middle, rest = split(line)
        tail = jnp.where(place == 0, head, jnp.where(place == 1, middle, rest)).astype(BF16)
        for c in range(pack_ref.shape[0]):
            pack_ref[c, :, depth:] = tail


def stage_kernel(data_ref, out_ref):
    parts, cores, blocks, part, depth = data_ref.shape
    for b in range(blocks):
        for s in range(parts):
            for k in range(cores):
                out_ref[b, s * part : (s + 1) * part, k * depth : (k + 1) * depth] = data_ref[s, k, b]


def plan_kernel(plan_ref, data_ref, out_ref):
    _, rows, _ = plan_ref.shape
    acc = jnp.zeros(out_ref.shape, F32)
    mass = jnp.zeros((rows, 1), F32)
    for c in range(plan_ref.shape[0]):
        plan = plan_ref[c]
        mass += jnp.sum(plan.astype(F32), axis=1, keepdims=True)
        acc += jnp.dot(plan, data_ref[c], preferred_element_type=F32)
    out_ref[...] = (acc / mass).astype(BF16)


def log_sum_exp(value, axis):
    peak = jnp.max(value, axis=axis, keepdims=True)
    return jnp.squeeze(peak, axis) + jnp.log(jnp.sum(jnp.exp(value - peak), axis=axis))


def body(noise, data):
    rows, width = noise.shape
    cols, depth = data.shape
    planes = ROWS // 2
    part = cols // planes
    log_rows = math.log(rows * ROWS)
    log_cols = math.log(cols * COLS)
    scale = -1.0 / (EPS * width * COLS)
    row = lax.axis_index("row").astype(jnp.int32)
    place = jnp.stack([lax.rem(row, 2), row // 2])

    data_all = lax.all_gather(data, "row", axis=0)
    noise_all = copies(noise.T, "col", COLS)
    noise_sq = jnp.sum(jnp.square(noise_all.astype(F32)), axis=(0, 1)).reshape(1, rows)
    data_all, noise_all, noise_sq = lax.optimization_barrier((data_all, noise_all, noise_sq))

    some = COLS // GRID
    cost, pack = pl.pallas_call(
        functools.partial(cost_kernel, scale),
        out_shape=[
            jax.ShapeDtypeStruct((rows, cols), F32),
            jax.ShapeDtypeStruct((COLS, part, depth + rows), BF16),
        ],
        grid_spec=pltpu.PrefetchScalarGridSpec(
            num_scalar_prefetch=1,
            grid=(GRID,),
            in_specs=[
                VM,
                pl.BlockSpec((2 * some, cols, depth), lambda c, place: (c, 0, 0)),
                pl.BlockSpec((1, rows), lambda c, place: (0, 0)),
            ],
            out_specs=[
                pl.BlockSpec((rows, cols), lambda c, place: (0, 0)),
                pl.BlockSpec((COLS, part, depth + rows), lambda c, place: (0, 0, 0)),
            ],
            scratch_shapes=[
                pltpu.VMEM((cols, rows), F32),
                pltpu.VMEM((cols, 128), F32),
            ],
        ),
        compiler_params=pltpu.CompilerParams(vmem_limit_bytes=48 * MIB),
        cost_estimate=pl.CostEstimate(
            flops=2 * rows * cols * COLS * width, bytes_accessed=12 * MIB, transcendentals=0
        ),
        name="cost",
    )(place, noise_all, data_all, noise_sq)
    scores = cost * scale
    pack = lax.all_to_all(pack, "col", split_axis=0, concat_axis=0)
    parts = pack[:, :3, depth:].astype(F32).sum(axis=1)

    values = lax.all_gather(pack[:, :, :depth], "row", axis=0).reshape(planes, 2, COLS, part, depth)

    for step in range(ITERS):
        if step > 0:
            parts = copies(log_sum_exp(scores + v[None, :], 1).reshape(1, rows), "col", COLS)
        u = -log_rows - log_sum_exp(parts.reshape(COLS, rows), 0)
        local = log_sum_exp(scores + u[:, None], 0)
        parts = copies(local.reshape(1, cols), "row", ROWS)
        v = -log_cols - log_sum_exp(parts, 0).reshape(cols)

    plan = jnp.exp(scores + u[:, None] + v[None, :] + log_rows).astype(BF16)
    plan = jnp.broadcast_to(plan[None], (COLS, rows, cols))
    values, plan = lax.optimization_barrier((values, plan))
    plan = lax.all_to_all(plan, "col", split_axis=0, concat_axis=0)
    staged = pl.pallas_call(
        stage_kernel,
        grid=(GRID,),
        out_shape=jax.ShapeDtypeStruct((COLS, cols, width), BF16),
        in_specs=[pl.BlockSpec((planes, 2, some, part, depth), lambda c: (0, 0, c, 0, 0))],
        out_specs=pl.BlockSpec((some, cols, width), lambda c: (c, 0, 0)),
        compiler_params=pltpu.CompilerParams(vmem_limit_bytes=42 * MIB),
        cost_estimate=pl.CostEstimate(flops=0, bytes_accessed=16 * MIB, transcendentals=0),
        name="stage",
    )(values)
    targets = pl.pallas_call(
        plan_kernel,
        out_shape=jax.ShapeDtypeStruct((rows, width), BF16),
        in_specs=[VM, VM],
        out_specs=VM,
        compiler_params=pltpu.CompilerParams(vmem_limit_bytes=24 * MIB),
        name="plan",
    )(plan, staged)
    return (targets, EPS * u, EPS * v)


def solution(mesh):
    return jax.shard_map(
        body,
        mesh=mesh,
        in_specs=(P("row", "col"), P("col", "row")),
        out_specs=(P("row", "col"), P("row"), P("col")),
        check_vma=False,
    )
```

```python
import functools
import math

import jax
import jax.numpy as jnp
from jax import lax
from jax.experimental import pallas as pl
from jax.experimental.pallas import tpu as pltpu
from jax.sharding import PartitionSpec as P

ITERS = 3
EPS = 0.01
COLS = 16
ROWS = 32
F32 = jnp.float32
BF16 = jnp.bfloat16
PARTS = 8
MIB = 1024 * 1024
VM = pl.BlockSpec(memory_space=pltpu.VMEM)
SM = pl.BlockSpec(memory_space=pltpu.SMEM)
ANY = pl.BlockSpec(memory_space=pl.ANY)


def copies(value, axis, size):
    sent = jnp.broadcast_to(value[None], (size,) + value.shape)
    return lax.all_to_all(sent, axis, split_axis=0, concat_axis=0)


def fold(value):
    value = value.astype(F32)
    value = value * value
    parts = [value[..., k : k + 128] for k in range(0, value.shape[-1], 128)]
    while len(parts) > 1:
        parts = [parts[k] + parts[k + 1] for k in range(0, len(parts), 2)]
    return parts[0]


def split(value):
    parts = []
    for _ in range(2):
        far = value * 65537.0
        head = far - (far - value)
        parts.append(head)
        value = value - head
    return parts + [value]


def cost_kernel(scale, place_ref, noise_hbm, data_hbm, noise_sq_ref, cost_ref, pack_ref, noise_ref, data_ref, sems):
    core, plane = place_ref[0], place_ref[1]
    blocks, _, rows = noise_ref.shape
    _, cols, depth = data_ref.shape
    part = pack_ref.shape[1]
    some = blocks // PARTS
    copies_in = []
    for k in range(PARTS):
        pair = []
        for n, (source, target, size) in enumerate(((noise_hbm, noise_ref, some), (data_hbm, data_ref, 2 * some))):
            here = pl.ds(k * size, size)
            pair.append(pltpu.make_async_copy(source.at[here], target.at[here], sems.at[n, k]))
            pair[-1].start()
        copies_in.append(pair)

    share = pl.ds(pl.multiple_of(plane * part, part), part)
    dots = jnp.zeros((cols, rows), F32)
    data_sq = jnp.zeros((cols, 128), F32)
    for k in range(PARTS):
        for copy in copies_in[k]:
            copy.wait()
        for b in range(k * some, (k + 1) * some):
            for half in range(2):
                data = data_ref[2 * b + half]
                noise = noise_ref[b, half * depth : (half + 1) * depth, :]
                dots += jnp.dot(data, noise, preferred_element_type=F32)
                data_sq += fold(data)
            pack_ref[b, :, :depth] = data_ref[2 * b + core, share, :]

    squares = jnp.sum(data_sq, axis=1, keepdims=True) + noise_sq_ref[...]
    turned = squares - 2.0 * dots
    cost_ref[...] = turned.T
    scores = turned * scale
    peak = jnp.max(scores, axis=0, keepdims=True)
    local = peak + jnp.log(jnp.sum(jnp.exp(scores - peak), axis=0, keepdims=True))
    line = jnp.broadcast_to(local, (part, rows))
    place = lax.broadcasted_iota(jnp.int32, line.shape, 0)
    head, middle, rest = split(line)
    tail = jnp.where(place == 0, head, jnp.where(place == 1, middle, rest)).astype(BF16)
    for c in range(blocks):
        pack_ref[c, :, depth:] = tail


def plan_kernel(plan_ref, data_hbm, out_ref, data_ref, acc_ref, sems):
    parts, cores, blocks, _, width = data_ref.shape
    rows = plan_ref.shape[1]
    some = blocks // PARTS
    copies_in = []
    for k in range(PARTS):
        here = pl.ds(k * some, some)
        copies_in.append(pltpu.make_async_copy(data_hbm.at[:, :, here], data_ref.at[:, :, here], sems.at[k]))
        copies_in[-1].start()
    acc_ref[...] = jnp.zeros_like(acc_ref)
    mass = jnp.zeros((rows, 1), F32)
    for b in range(blocks):
        mass += jnp.sum(plan_ref[b].astype(F32), axis=1, keepdims=True)
    for k in range(PARTS):
        copies_in[k].wait()
        for b in range(k * some, (k + 1) * some):
            for c in range(cores):
                block = jnp.concatenate([data_ref[s, c, b] for s in range(parts)], axis=0)
                acc_ref[:, c * width : (c + 1) * width] += jnp.dot(plan_ref[b], block, preferred_element_type=F32)
    out_ref[...] = (acc_ref[...] / mass).astype(BF16)


def log_sum_exp(value, axis):
    peak = jnp.max(value, axis=axis, keepdims=True)
    return jnp.squeeze(peak, axis) + jnp.log(jnp.sum(jnp.exp(value - peak), axis=axis))


def body(noise, data):
    rows, width = noise.shape
    cols, depth = data.shape
    planes = ROWS // 2
    part = cols // planes
    log_rows = math.log(rows * ROWS)
    log_cols = math.log(cols * COLS)
    scale = -1.0 / (EPS * width * COLS)
    row = lax.axis_index("row").astype(jnp.int32)
    place = jnp.stack([lax.rem(row, 2), row // 2])

    data_all = lax.all_gather(data, "row", axis=0)
    noise_all = copies(noise.T, "col", COLS)
    noise_sq = jnp.sum(jnp.square(noise_all.astype(F32)), axis=(0, 1)).reshape(1, rows)
    data_all, noise_all, noise_sq = lax.optimization_barrier((data_all, noise_all, noise_sq))

    cost, pack = pl.pallas_call(
        functools.partial(cost_kernel, scale),
        out_shape=[
            jax.ShapeDtypeStruct((rows, cols), F32),
            jax.ShapeDtypeStruct((COLS, part, depth + rows), BF16),
        ],
        in_specs=[SM, ANY, ANY, VM],
        out_specs=[VM, VM],
        scratch_shapes=[
            pltpu.VMEM((COLS, width, rows), BF16),
            pltpu.VMEM((2 * COLS, cols, depth), BF16),
            pltpu.SemaphoreType.DMA((2, PARTS)),
        ],
        compiler_params=pltpu.CompilerParams(vmem_limit_bytes=50 * MIB),
        cost_estimate=pl.CostEstimate(
            flops=2 * rows * cols * COLS * width, bytes_accessed=12 * MIB, transcendentals=0
        ),
        name="cost",
    )(place, noise_all, data_all, noise_sq)
    scores = cost * scale
    pack = lax.all_to_all(pack, "col", split_axis=0, concat_axis=0)
    parts = pack[:, :3, depth:].astype(F32).sum(axis=1)

    values = lax.all_gather(pack[:, :, :depth], "row", axis=0).reshape(planes, 2, COLS, part, depth)

    for step in range(ITERS):
        if step > 0:
            parts = copies(log_sum_exp(scores + v[None, :], 1).reshape(1, rows), "col", COLS)
        u = -log_rows - log_sum_exp(parts.reshape(COLS, rows), 0)
        local = log_sum_exp(scores + u[:, None], 0)
        parts = copies(local.reshape(1, cols), "row", ROWS)
        v = -log_cols - log_sum_exp(parts, 0).reshape(cols)

    values, v = lax.optimization_barrier((values, v))
    plan = jnp.exp(scores + u[:, None] + v[None, :] + log_rows).astype(BF16)
    plan = copies(plan, "col", COLS)
    targets = pl.pallas_call(
        plan_kernel,
        out_shape=jax.ShapeDtypeStruct((rows, width), BF16),
        in_specs=[VM, ANY],
        out_specs=VM,
        scratch_shapes=[
            pltpu.VMEM((planes, 2, COLS, part, depth), BF16),
            pltpu.VMEM((rows, width), F32),
            pltpu.SemaphoreType.DMA((PARTS,)),
        ],
        compiler_params=pltpu.CompilerParams(vmem_limit_bytes=50 * MIB),
        name="plan",
    )(plan, values)
    return (targets, EPS * u, EPS * v)


def solution(mesh):
    return jax.shard_map(
        body,
        mesh=mesh,
        in_specs=(P("row", "col"), P("col", "row")),
        out_specs=(P("row", "col"), P("row"), P("col")),
        check_vma=False,
    )
```

```python
import functools
import math

import jax
import jax.numpy as jnp
from jax import lax
from jax.experimental import pallas as pl
from jax.experimental.pallas import tpu as pltpu
from jax.sharding import PartitionSpec as P

ITERS = 3
EPS = 0.01
COLS = 16
ROWS = 32
F32 = jnp.float32
BF16 = jnp.bfloat16
PARTS = 8
MIB = 1024 * 1024
VM = pl.BlockSpec(memory_space=pltpu.VMEM)
SM = pl.BlockSpec(memory_space=pltpu.SMEM)
ANY = pl.BlockSpec(memory_space=pl.ANY)


def copies(value, axis, size):
    sent = jnp.broadcast_to(value[None], (size,) + value.shape)
    return lax.all_to_all(sent, axis, split_axis=0, concat_axis=0)


def fold(value):
    value = value.astype(F32)
    value = value * value
    parts = [value[..., k : k + 128] for k in range(0, value.shape[-1], 128)]
    while len(parts) > 1:
        parts = [parts[k] + parts[k + 1] for k in range(0, len(parts), 2)]
    return parts[0]


def split(value):
    parts = []
    for _ in range(2):
        far = value * 65537.0
        head = far - (far - value)
        parts.append(head)
        value = value - head
    return parts + [value]


def cost_kernel(scale, place_ref, noise_hbm, data_hbm, noise_sq_ref, cost_ref, pack_ref, noise_ref, data_ref, sems):
    core, plane = place_ref[0], place_ref[1]
    blocks, _, rows = noise_ref.shape
    _, cols, depth = data_ref.shape
    part = pack_ref.shape[1]
    some = blocks // PARTS
    copies_in = []
    for k in range(PARTS):
        pair = []
        for n, (source, target, size) in enumerate(((noise_hbm, noise_ref, some), (data_hbm, data_ref, 2 * some))):
            here = pl.ds(k * size, size)
            pair.append(pltpu.make_async_copy(source.at[here], target.at[here], sems.at[n, k]))
            pair[-1].start()
        copies_in.append(pair)

    share = pl.ds(pl.multiple_of(plane * part, part), part)
    dots = jnp.zeros((cols, rows), F32)
    data_sq = jnp.zeros((cols, 128), F32)
    for k in range(PARTS):
        for copy in copies_in[k]:
            copy.wait()
        for b in range(k * some, (k + 1) * some):
            for half in range(2):
                data = data_ref[2 * b + half]
                noise = noise_ref[b, half * depth : (half + 1) * depth, :]
                dots += jnp.dot(data, noise, preferred_element_type=F32)
                data_sq += fold(data)
            pack_ref[b, :, :depth] = data_ref[2 * b + core, share, :]

    squares = jnp.sum(data_sq, axis=1, keepdims=True) + noise_sq_ref[...]
    turned = squares - 2.0 * dots
    cost_ref[...] = turned.T
    scores = turned * scale
    peak = jnp.max(scores, axis=0, keepdims=True)
    local = peak + jnp.log(jnp.sum(jnp.exp(scores - peak), axis=0, keepdims=True))
    line = jnp.broadcast_to(local, (part, rows))
    place = lax.broadcasted_iota(jnp.int32, line.shape, 0)
    head, middle, rest = split(line)
    tail = jnp.where(place == 0, head, jnp.where(place == 1, middle, rest)).astype(BF16)
    for c in range(blocks):
        pack_ref[c, :, depth:] = tail


def plan_kernel(plan_ref, data_hbm, out_ref, data_ref, acc_ref, sems):
    parts, cores, blocks, _, width = data_ref.shape
    rows = plan_ref.shape[1]
    some = blocks // PARTS
    copies_in = []
    for k in range(PARTS):
        here = pl.ds(k * some, some)
        source = data_hbm.at[:, :, here, :, pl.ds(0, width)]
        copies_in.append(pltpu.make_async_copy(source, data_ref.at[:, :, here], sems.at[k]))
        copies_in[-1].start()
    acc_ref[...] = jnp.zeros_like(acc_ref)
    mass = jnp.zeros((rows, 1), F32)
    for b in range(blocks):
        mass += jnp.sum(plan_ref[b].astype(F32), axis=1, keepdims=True)
    for k in range(PARTS):
        copies_in[k].wait()
        for b in range(k * some, (k + 1) * some):
            for c in range(cores):
                block = jnp.concatenate([data_ref[s, c, b] for s in range(parts)], axis=0)
                acc_ref[:, c * width : (c + 1) * width] += jnp.dot(plan_ref[b], block, preferred_element_type=F32)
    out_ref[...] = (acc_ref[...] / mass).astype(BF16)


def log_sum_exp(value, axis):
    peak = jnp.max(value, axis=axis, keepdims=True)
    return jnp.squeeze(peak, axis) + jnp.log(jnp.sum(jnp.exp(value - peak), axis=axis))


def body(noise, data):
    rows, width = noise.shape
    cols, depth = data.shape
    planes = ROWS // 2
    part = cols // planes
    log_rows = math.log(rows * ROWS)
    log_cols = math.log(cols * COLS)
    scale = -1.0 / (EPS * width * COLS)
    row = lax.axis_index("row").astype(jnp.int32)
    place = jnp.stack([lax.rem(row, 2), row // 2])

    data_all = lax.all_gather(data, "row", axis=0)
    noise_all = copies(noise.T, "col", COLS)
    noise_sq = jnp.sum(jnp.square(noise_all.astype(F32)), axis=(0, 1)).reshape(1, rows)
    data_all, noise_all, noise_sq = lax.optimization_barrier((data_all, noise_all, noise_sq))

    cost, pack = pl.pallas_call(
        functools.partial(cost_kernel, scale),
        out_shape=[
            jax.ShapeDtypeStruct((rows, cols), F32),
            jax.ShapeDtypeStruct((COLS, part, depth + rows), BF16),
        ],
        in_specs=[SM, ANY, ANY, VM],
        out_specs=[VM, VM],
        scratch_shapes=[
            pltpu.VMEM((COLS, width, rows), BF16),
            pltpu.VMEM((2 * COLS, cols, depth), BF16),
            pltpu.SemaphoreType.DMA((2, PARTS)),
        ],
        compiler_params=pltpu.CompilerParams(vmem_limit_bytes=50 * MIB),
        cost_estimate=pl.CostEstimate(
            flops=2 * rows * cols * COLS * width, bytes_accessed=12 * MIB, transcendentals=0
        ),
        name="cost",
    )(place, noise_all, data_all, noise_sq)
    scores = cost * scale
    pack = lax.all_to_all(pack, "col", split_axis=0, concat_axis=0)
    parts = pack[:, :3, depth:].astype(F32).sum(axis=1)

    values = lax.all_gather(pack, "row", axis=0).reshape(planes, 2, COLS, part, depth + rows)

    for step in range(ITERS):
        if step > 0:
            parts = copies(log_sum_exp(scores + v[None, :], 1).reshape(1, rows), "col", COLS)
        u = -log_rows - log_sum_exp(parts.reshape(COLS, rows), 0)
        local = log_sum_exp(scores + u[:, None], 0)
        parts = copies(local.reshape(1, cols), "row", ROWS)
        v = -log_cols - log_sum_exp(parts, 0).reshape(cols)

    plan = jnp.exp(scores + u[:, None] + v[None, :] + log_rows).astype(BF16)
    plan = jnp.broadcast_to(plan[None], (COLS, rows, cols))
    values, _ = lax.optimization_barrier((values, plan))
    plan = lax.all_to_all(plan, "col", split_axis=0, concat_axis=0)
    targets = pl.pallas_call(
        plan_kernel,
        out_shape=jax.ShapeDtypeStruct((rows, width), BF16),
        in_specs=[VM, ANY],
        out_specs=VM,
        scratch_shapes=[
            pltpu.VMEM((planes, 2, COLS, part, depth), BF16),
            pltpu.VMEM((rows, width), F32),
            pltpu.SemaphoreType.DMA((PARTS,)),
        ],
        compiler_params=pltpu.CompilerParams(vmem_limit_bytes=50 * MIB),
        name="plan",
    )(plan, values)
    return (targets, EPS * u, EPS * v)


def solution(mesh):
    return jax.shard_map(
        body,
        mesh=mesh,
        in_specs=(P("row", "col"), P("col", "row")),
        out_specs=(P("row", "col"), P("row"), P("col")),
        check_vma=False,
    )
```

```python
import functools
import math

import jax
import jax.numpy as jnp
from jax import lax
from jax.experimental import pallas as pl
from jax.experimental.pallas import tpu as pltpu
from jax.sharding import PartitionSpec as P

ITERS = 3
EPS = 0.01
COLS = 16
ROWS = 32
F32 = jnp.float32
BF16 = jnp.bfloat16
PARTS = 8
MIB = 1024 * 1024
VM = pl.BlockSpec(memory_space=pltpu.VMEM)
SM = pl.BlockSpec(memory_space=pltpu.SMEM)
ANY = pl.BlockSpec(memory_space=pl.ANY)


def copies(value, axis, size):
    sent = jnp.broadcast_to(value[None], (size,) + value.shape)
    return lax.all_to_all(sent, axis, split_axis=0, concat_axis=0)


def fold(value):
    value = value.astype(F32)
    value = value * value
    parts = [value[..., k : k + 128] for k in range(0, value.shape[-1], 128)]
    while len(parts) > 1:
        parts = [parts[k] + parts[k + 1] for k in range(0, len(parts), 2)]
    return parts[0]


def split(value):
    parts = []
    for _ in range(2):
        far = value * 65537.0
        head = far - (far - value)
        parts.append(head)
        value = value - head
    return parts + [value]


def cost_kernel(scale, place_ref, noise_hbm, data_hbm, noise_sq_ref, cost_ref, pack_ref, noise_ref, data_ref, sems):
    core, plane = place_ref[0], place_ref[1]
    blocks, _, rows = noise_ref.shape
    _, cols, depth = data_ref.shape
    part = pack_ref.shape[1]
    some = blocks // PARTS
    copies_in = []
    for k in range(PARTS):
        pair = []
        for n, (source, target, size) in enumerate(((noise_hbm, noise_ref, some), (data_hbm, data_ref, 2 * some))):
            here = pl.ds(k * size, size)
            pair.append(pltpu.make_async_copy(source.at[here], target.at[here], sems.at[n, k]))
            pair[-1].start()
        copies_in.append(pair)

    share = pl.ds(pl.multiple_of(plane * part, part), part)
    dots = jnp.zeros((cols, rows), F32)
    data_sq = jnp.zeros((cols, 128), F32)
    for k in range(PARTS):
        for copy in copies_in[k]:
            copy.wait()
        for b in range(k * some, (k + 1) * some):
            for half in range(2):
                data = data_ref[2 * b + half]
                noise = noise_ref[b, half * depth : (half + 1) * depth, :]
                dots += jnp.dot(data, noise, preferred_element_type=F32)
                data_sq += fold(data)
            pack_ref[b, :, :depth] = data_ref[2 * b + core, share, :]

    squares = jnp.sum(data_sq, axis=1, keepdims=True) + noise_sq_ref[...]
    turned = squares - 2.0 * dots
    cost_ref[...] = turned.T
    scores = turned * scale
    peak = jnp.max(scores, axis=0, keepdims=True)
    local = peak + jnp.log(jnp.sum(jnp.exp(scores - peak), axis=0, keepdims=True))
    line = jnp.broadcast_to(local, (part, rows))
    place = lax.broadcasted_iota(jnp.int32, line.shape, 0)
    head, middle, rest = split(line)
    tail = jnp.where(place == 0, head, jnp.where(place == 1, middle, rest)).astype(BF16)
    for c in range(blocks):
        pack_ref[c, :, depth:] = tail


def spread_kernel(scale, shift, cost_ref, u_ref, v_ref, out_ref):
    rows, cols = cost_ref.shape
    u = jnp.broadcast_to(u_ref[...], (rows, rows)).T
    u = jnp.concatenate([u] * (cols // rows), axis=1)
    plan = jnp.exp(cost_ref[...] * scale + u + v_ref[...] + shift).astype(BF16)
    for c in range(out_ref.shape[0]):
        out_ref[c] = plan


def plan_kernel(plan_ref, data_hbm, out_ref, data_ref, acc_ref, sems):
    parts, cores, blocks, _, width = data_ref.shape
    rows = plan_ref.shape[1]
    some = blocks // PARTS
    copies_in = []
    for k in range(PARTS):
        here = pl.ds(k * some, some)
        source = data_hbm.at[:, :, here, :, pl.ds(0, width)]
        copies_in.append(pltpu.make_async_copy(source, data_ref.at[:, :, here], sems.at[k]))
        copies_in[-1].start()
    acc_ref[...] = jnp.zeros_like(acc_ref)
    mass = jnp.zeros((rows, 1), F32)
    for b in range(blocks):
        mass += jnp.sum(plan_ref[b].astype(F32), axis=1, keepdims=True)
    for k in range(PARTS):
        copies_in[k].wait()
        for b in range(k * some, (k + 1) * some):
            for c in range(cores):
                block = jnp.concatenate([data_ref[s, c, b] for s in range(parts)], axis=0)
                acc_ref[:, c * width : (c + 1) * width] += jnp.dot(plan_ref[b], block, preferred_element_type=F32)
    out_ref[...] = (acc_ref[...] / mass).astype(BF16)


def log_sum_exp(value, axis):
    peak = jnp.max(value, axis=axis, keepdims=True)
    return jnp.squeeze(peak, axis) + jnp.log(jnp.sum(jnp.exp(value - peak), axis=axis))


def body(noise, data):
    rows, width = noise.shape
    cols, depth = data.shape
    planes = ROWS // 2
    part = cols // planes
    log_rows = math.log(rows * ROWS)
    log_cols = math.log(cols * COLS)
    scale = -1.0 / (EPS * width * COLS)
    row = lax.axis_index("row").astype(jnp.int32)
    place = jnp.stack([lax.rem(row, 2), row // 2])

    data_all = lax.all_gather(data, "row", axis=0)
    noise_all = copies(noise.T, "col", COLS)
    noise_sq = jnp.sum(jnp.square(noise_all.astype(F32)), axis=(0, 1)).reshape(1, rows)
    data_all, noise_all, noise_sq = lax.optimization_barrier((data_all, noise_all, noise_sq))

    cost, pack = pl.pallas_call(
        functools.partial(cost_kernel, scale),
        out_shape=[
            jax.ShapeDtypeStruct((rows, cols), F32),
            jax.ShapeDtypeStruct((COLS, part, depth + rows), BF16),
        ],
        in_specs=[SM, ANY, ANY, VM],
        out_specs=[VM, VM],
        scratch_shapes=[
            pltpu.VMEM((COLS, width, rows), BF16),
            pltpu.VMEM((2 * COLS, cols, depth), BF16),
            pltpu.SemaphoreType.DMA((2, PARTS)),
        ],
        compiler_params=pltpu.CompilerParams(vmem_limit_bytes=50 * MIB),
        cost_estimate=pl.CostEstimate(
            flops=2 * rows * cols * COLS * width, bytes_accessed=12 * MIB, transcendentals=0
        ),
        name="cost",
    )(place, noise_all, data_all, noise_sq)
    scores = cost * scale
    pack = lax.all_to_all(pack, "col", split_axis=0, concat_axis=0)
    parts = pack[:, :3, depth:].astype(F32).sum(axis=1)

    values = lax.all_gather(pack, "row", axis=0).reshape(planes, 2, COLS, part, depth + rows)

    for step in range(ITERS):
        if step > 0:
            parts = copies(log_sum_exp(scores + v[None, :], 1).reshape(1, rows), "col", COLS)
        u = -log_rows - log_sum_exp(parts.reshape(COLS, rows), 0)
        local = log_sum_exp(scores + u[:, None], 0)
        parts = copies(local.reshape(1, cols), "row", ROWS)
        v = -log_cols - log_sum_exp(parts, 0).reshape(cols)

    plan = pl.pallas_call(
        functools.partial(spread_kernel, scale, log_rows),
        out_shape=jax.ShapeDtypeStruct((COLS, rows, cols), BF16),
        in_specs=[VM] * 3,
        out_specs=VM,
        compiler_params=pltpu.CompilerParams(vmem_limit_bytes=16 * MIB),
        name="spread",
    )(cost, u.reshape(1, rows), v.reshape(1, cols))
    values, _ = lax.optimization_barrier((values, plan))
    plan = lax.all_to_all(plan, "col", split_axis=0, concat_axis=0)
    targets = pl.pallas_call(
        plan_kernel,
        out_shape=jax.ShapeDtypeStruct((rows, width), BF16),
        in_specs=[VM, ANY],
        out_specs=VM,
        scratch_shapes=[
            pltpu.VMEM((planes, 2, COLS, part, depth), BF16),
            pltpu.VMEM((rows, width), F32),
            pltpu.SemaphoreType.DMA((PARTS,)),
        ],
        compiler_params=pltpu.CompilerParams(vmem_limit_bytes=50 * MIB),
        name="plan",
    )(plan, values)
    return (targets, EPS * u, EPS * v)


def solution(mesh):
    return jax.shard_map(
        body,
        mesh=mesh,
        in_specs=(P("row", "col"), P("col", "row")),
        out_specs=(P("row", "col"), P("row"), P("col")),
        check_vma=False,
    )
```

```python
import functools
import math

import jax
import jax.numpy as jnp
from jax import lax
from jax.experimental import pallas as pl
from jax.experimental.pallas import tpu as pltpu
from jax.sharding import PartitionSpec as P

ITERS = 3
EPS = 0.01
COLS = 16
ROWS = 32
F32 = jnp.float32
BF16 = jnp.bfloat16
PARTS = 8
MIB = 1024 * 1024
VM = pl.BlockSpec(memory_space=pltpu.VMEM)
SM = pl.BlockSpec(memory_space=pltpu.SMEM)
ANY = pl.BlockSpec(memory_space=pl.ANY)


def copies(value, axis, size):
    sent = jnp.broadcast_to(value[None], (size,) + value.shape)
    return lax.all_to_all(sent, axis, split_axis=0, concat_axis=0)


def fold(value):
    value = value.astype(F32)
    value = value * value
    parts = [value[..., k : k + 128] for k in range(0, value.shape[-1], 128)]
    while len(parts) > 1:
        parts = [parts[k] + parts[k + 1] for k in range(0, len(parts), 2)]
    return parts[0]


def split(value):
    parts = []
    for _ in range(2):
        far = value * 65537.0
        head = far - (far - value)
        parts.append(head)
        value = value - head
    return parts + [value]


def cost_kernel(scale, place_ref, noise_hbm, data_hbm, noise_sq_ref, cost_ref, pack_ref, noise_ref, data_ref, sems):
    core, plane = place_ref[0], place_ref[1]
    blocks, _, rows = noise_ref.shape
    _, cols, depth = data_ref.shape
    part = pack_ref.shape[1]
    some = blocks // PARTS
    copies_in = []
    for k in range(PARTS):
        pair = []
        for n, (source, target, size) in enumerate(((noise_hbm, noise_ref, some), (data_hbm, data_ref, 2 * some))):
            here = pl.ds(k * size, size)
            pair.append(pltpu.make_async_copy(source.at[here], target.at[here], sems.at[n, k]))
            pair[-1].start()
        copies_in.append(pair)

    share = pl.ds(pl.multiple_of(plane * part, part), part)
    dots = jnp.zeros((cols, rows), F32)
    data_sq = jnp.zeros((cols, 128), F32)
    for k in range(PARTS):
        for copy in copies_in[k]:
            copy.wait()
        for b in range(k * some, (k + 1) * some):
            for half in range(2):
                data = data_ref[2 * b + half]
                noise = noise_ref[b, half * depth : (half + 1) * depth, :]
                dots += jnp.dot(data, noise, preferred_element_type=F32)
                data_sq += fold(data)
            pack_ref[b, :, :depth] = data_ref[2 * b + core, share, :]

    squares = jnp.sum(data_sq, axis=1, keepdims=True) + noise_sq_ref[...]
    turned = squares - 2.0 * dots
    cost_ref[...] = turned.T
    scores = turned * scale
    peak = jnp.max(scores, axis=0, keepdims=True)
    local = peak + jnp.log(jnp.sum(jnp.exp(scores - peak), axis=0, keepdims=True))
    line = jnp.broadcast_to(local, (part, rows))
    place = lax.broadcasted_iota(jnp.int32, line.shape, 0)
    head, middle, rest = split(line)
    tail = jnp.where(place == 0, head, jnp.where(place == 1, middle, rest)).astype(BF16)
    for c in range(blocks):
        pack_ref[c, :, depth:] = tail


def spread_kernel(scale, shift, cost_ref, u_ref, v_ref, out_ref, row_ref, col_ref):
    row_ref[...] = EPS * u_ref[...]
    col_ref[...] = EPS * v_ref[...]
    rows, cols = cost_ref.shape
    u = jnp.broadcast_to(u_ref[...], (rows, rows)).T
    u = jnp.concatenate([u] * (cols // rows), axis=1)
    plan = jnp.exp(cost_ref[...] * scale + u + v_ref[...] + shift).astype(BF16)
    for c in range(out_ref.shape[0]):
        out_ref[c] = plan


def plan_kernel(plan_ref, data_hbm, out_ref, data_ref, acc_ref, sems):
    parts, cores, blocks, _, width = data_ref.shape
    rows = plan_ref.shape[1]
    some = blocks // PARTS
    copies_in = []
    for k in range(PARTS):
        here = pl.ds(k * some, some)
        source = data_hbm.at[:, :, here, :, pl.ds(0, width)]
        copies_in.append(pltpu.make_async_copy(source, data_ref.at[:, :, here], sems.at[k]))
        copies_in[-1].start()
    acc_ref[...] = jnp.zeros_like(acc_ref)
    mass = jnp.zeros((rows, 1), F32)
    for b in range(blocks):
        mass += jnp.sum(plan_ref[b].astype(F32), axis=1, keepdims=True)
    for k in range(PARTS):
        copies_in[k].wait()
        for b in range(k * some, (k + 1) * some):
            for c in range(cores):
                block = jnp.concatenate([data_ref[s, c, b] for s in range(parts)], axis=0)
                acc_ref[:, c * width : (c + 1) * width] += jnp.dot(plan_ref[b], block, preferred_element_type=F32)
    out_ref[...] = (acc_ref[...] / mass).astype(BF16)


def log_sum_exp(value, axis):
    peak = jnp.max(value, axis=axis, keepdims=True)
    return jnp.squeeze(peak, axis) + jnp.log(jnp.sum(jnp.exp(value - peak), axis=axis))


def body(noise, data):
    rows, width = noise.shape
    cols, depth = data.shape
    planes = ROWS // 2
    part = cols // planes
    log_rows = math.log(rows * ROWS)
    log_cols = math.log(cols * COLS)
    scale = -1.0 / (EPS * width * COLS)
    row = lax.axis_index("row").astype(jnp.int32)
    place = jnp.stack([lax.rem(row, 2), row // 2])

    data_all = lax.all_gather(data, "row", axis=0)
    noise_all = copies(noise.T, "col", COLS)
    noise_sq = jnp.sum(jnp.square(noise_all.astype(F32)), axis=(0, 1)).reshape(1, rows)
    data_all, noise_all, noise_sq = lax.optimization_barrier((data_all, noise_all, noise_sq))

    cost, pack = pl.pallas_call(
        functools.partial(cost_kernel, scale),
        out_shape=[
            jax.ShapeDtypeStruct((rows, cols), F32),
            jax.ShapeDtypeStruct((COLS, part, depth + rows), BF16),
        ],
        in_specs=[SM, ANY, ANY, VM],
        out_specs=[VM, VM],
        scratch_shapes=[
            pltpu.VMEM((COLS, width, rows), BF16),
            pltpu.VMEM((2 * COLS, cols, depth), BF16),
            pltpu.SemaphoreType.DMA((2, PARTS)),
        ],
        compiler_params=pltpu.CompilerParams(vmem_limit_bytes=50 * MIB),
        cost_estimate=pl.CostEstimate(
            flops=2 * rows * cols * COLS * width, bytes_accessed=12 * MIB, transcendentals=0
        ),
        name="cost",
    )(place, noise_all, data_all, noise_sq)
    scores = cost * scale
    pack = lax.all_to_all(pack, "col", split_axis=0, concat_axis=0)
    parts = pack[:, :3, depth:].astype(F32).sum(axis=1)

    values = lax.all_gather(pack, "row", axis=0).reshape(planes, 2, COLS, part, depth + rows)

    for step in range(ITERS):
        if step > 0:
            parts = copies(log_sum_exp(scores + v[None, :], 1).reshape(1, rows), "col", COLS)
        u = -log_rows - log_sum_exp(parts.reshape(COLS, rows), 0)
        local = log_sum_exp(scores + u[:, None], 0)
        parts = copies(local.reshape(1, cols), "row", ROWS)
        v = -log_cols - log_sum_exp(parts, 0).reshape(cols)

    plan, row_potential, col_potential = pl.pallas_call(
        functools.partial(spread_kernel, scale, log_rows),
        out_shape=[
            jax.ShapeDtypeStruct((COLS, rows, cols), BF16),
            jax.ShapeDtypeStruct((1, rows), F32),
            jax.ShapeDtypeStruct((1, cols), F32),
        ],
        in_specs=[VM] * 3,
        out_specs=[VM] * 3,
        compiler_params=pltpu.CompilerParams(vmem_limit_bytes=16 * MIB),
        name="spread",
    )(cost, u.reshape(1, rows), v.reshape(1, cols))
    values, _ = lax.optimization_barrier((values, plan))
    plan = lax.all_to_all(plan, "col", split_axis=0, concat_axis=0)
    targets = pl.pallas_call(
        plan_kernel,
        out_shape=jax.ShapeDtypeStruct((rows, width), BF16),
        in_specs=[VM, ANY],
        out_specs=VM,
        scratch_shapes=[
            pltpu.VMEM((planes, 2, COLS, part, depth), BF16),
            pltpu.VMEM((rows, width), F32),
            pltpu.SemaphoreType.DMA((PARTS,)),
        ],
        compiler_params=pltpu.CompilerParams(vmem_limit_bytes=50 * MIB),
        name="plan",
    )(plan, values)
    return (targets, row_potential.reshape(rows), col_potential.reshape(cols))


def solution(mesh):
    return jax.shard_map(
        body,
        mesh=mesh,
        in_specs=(P("row", "col"), P("col", "row")),
        out_specs=(P("row", "col"), P("row"), P("col")),
        check_vma=False,
    )
```
